256 devices in a mesh: ctx: 8 (over x_hi, y), exp: 32 (over z, x_lo, core).
Axes of the slice: x: 4 (x_hi: 2, x_lo: 2; x = x_hi * 2 + x_lo), y: 4, z: 8, core: 2. Of those that a mesh axis runs over, the one named last changes fastest.
Arguments:
- stream_in: bfloat16 [2048, 4096], P(('ctx', 'exp')), may hold values from -4 to 4
- queries: bfloat16 [2048, 4096], P('ctx', 'exp')
- keys: bfloat16 [2048, 4096], P('ctx', 'exp')
- values: bfloat16 [2048, 4096], P('ctx', 'exp'), may hold values from -6 to 6
- w_out: bfloat16 [4096, 4096], P('exp'), may hold values from -0.5 to 0.5
- norm_gain: float32 [4096], replicated, may hold values from 0.25 to 1.75
- expert_ids: int32 [2048, 6], P(('ctx', 'exp')), may hold values from 0 to 63, all different within a row; in each aligned block of 8 rows (0 to 7, 8 to 15, ...) at most 2 rows name the same one
- gates: float32 [2048, 6], P(('ctx', 'exp')), may hold values from 0.1 to 1
- w_gate: bfloat16 [8, 32, 352, 4096], P('ctx', 'exp'), may hold values from -0.09375 to 0.09375
- w_up: bfloat16 [8, 32, 352, 4096], P('ctx', 'exp'), may hold values from -0.09375 to 0.09375
- w_down: bfloat16 [8, 32, 352, 4096], P('ctx', 'exp'), may hold values from -0.15625 to 0.15625
Outputs:
- layer_out: bfloat16 [2048, 4096], P(('ctx', 'exp'))
The draws below stay inside these ranges and needn't reach their ends.
Inputs may be any that keep to these rules, and one draw needn't show every extreme that they name: `expert_ids`: among the 8 tokens of one device (aligned blocks of rows), no expert is named by more than 2 of them; in every draw some expert is named by exactly 2 in some block.
All inputs are finite; a program needn't handle non-finite values.
Results may differ from the reference program's by a relative error of at most 0.03.
Values may be sent and summed in bfloat16 or wider, within the bound.
No kernel may reach another device: no remote copies, remote signals or barrier semaphores. Data moves between devices by JAX's collectives and lax.ppermute only.
A program may use at most 128 MiB of HBM per device.

```python
import math
import jax
import jax.numpy as jnp
import numpy as np
from jax import lax

D = 4096
HEAD_DIM = 128
FF_EXP = 1408
TOPK = 6
PIECES = 4
TOK_DEV = 8
HEADS = 32
EXPERTS = 64
CAP = 2
SHARD = 256
SEQ = 2048
N_CTX = 8
N_EXP = 32


def shared_base(key):
    return jax.random.normal(key, (SEQ, HEADS * HEAD_DIM), jnp.float32)


def draw_keys(key, part):
    base = shared_base(key)
    return base.astype(jnp.bfloat16)


def draw_queries(key, part):
    key = jax.random.fold_in(key, 7)
    fresh = jax.random.normal(key, (SEQ, HEADS * HEAD_DIM), jnp.float32)
    return fresh.astype(jnp.bfloat16)


def block_scale(rng, shape, cuts, low, top_value):
    def one(axis_at, parts):
        steps = jax.random.uniform(jax.random.fold_in(jax.random.fold_in(rng, 6), axis_at), (parts,), jnp.float32, low / len(cuts), top_value / len(cuts))
        return jnp.repeat(jnp.exp(steps), shape[axis_at] // parts).reshape((-1,) + (1,) * (len(shape) - axis_at - 1))

    factor_of = one(*cuts[0])
    for cut in cuts[1:]:
        factor_of = factor_of * one(*cut)
    return factor_of


def assign_block(own_key, own, number, rows, count, top, limit, lean):
    sequence = jax.random.permutation(own_key, count)
    heavy_load, usual = shares(count, rows * top, limit, lean, True), shares(count, rows * top, limit, lean, False)
    places = jnp.arange(count)

    def named(tallies, turn):
        used = int((tallies > 0).sum())
        fixed = max(1, used // 4)
        shifted = fixed + (places - fixed + turn * (used - fixed)) % max(1, count - fixed)
        return jnp.zeros((count,), jnp.int32).at[sequence[jnp.where(places < fixed, places, shifted)]].set(jnp.asarray(tallies, jnp.int32))

    tallies = jnp.where(number % 4 == 0, named(heavy_load, number // 4), named(usual, number - number // 4 - 1))
    mixed = jax.random.permutation(jax.random.fold_in(own, 3), count)
    donor, receiver = mixed[0:count // 2 * 2:2], mixed[1:count // 2 * 2:2]
    room = jnp.minimum(tallies[donor] - 1, limit - tallies[receiver]) // 2
    room = jnp.where((donor == sequence[0]) | (receiver == sequence[0]) | (tallies[receiver] == 0), 0, jnp.maximum(room, 0))
    shifted = jax.random.randint(jax.random.fold_in(own, 4), (count // 2,), 0, 1 << 20) % (room + 1)
    tallies = tallies.at[donor].add(-shifted).at[receiver].add(shifted)
    members = jnp.searchsorted(jnp.cumsum(tallies), jnp.arange(rows * top), side="right").astype(jnp.int32)
    grid = members.reshape(top, rows).T
    grid = grid[jax.random.permutation(jax.random.fold_in(own, 1), rows)]
    turn = jax.random.randint(jax.random.fold_in(own, 2), (rows, 1), 0, top)
    return jnp.take_along_axis(grid, (jnp.arange(top)[None, :] + turn) % top, axis=1)


def shares(amount, total, reach, lean, full):
    loads = [(1 << 20) // math.isqrt(standing ** lean) + 1 for standing in range(1, amount + 1)]
    largest = reach if full else min(reach, max(-(-total // amount), total * loads[0] // sum(loads)))
    least = 1 if total - largest >= amount - 1 else 0
    given, spare = [largest] + [least] * (amount - 1), total - largest - least * (amount - 1)
    while spare > 0:
        movable = [i for i in range(1, amount) if given[i] < largest] or [i for i in range(1, amount) if given[i] < reach]
        pool, remaining = sum([loads[i] for i in movable]), spare
        for i in movable:
            extra = min(reach - given[i], max(1, remaining * loads[i] // pool), spare)
            given[i] = given[i] + extra
            spare = spare - extra
    return np.array(given)


def gaussian(key, dims, spread, most, shards=(), held_as=jnp.bfloat16):
    values = jax.random.normal(key, dims, jnp.float32) * spread
    if len(shards) > 0:
        values = block_scale(key, dims, shards, -0.22, 0.18) * values
    return jnp.clip(values, min=-most, max=most).astype(held_as)


def setup_inputs(seed: int = 0) -> dict:
    key_of = jax.random.split(jax.random.key(seed), 12)
    stream_in = gaussian(key_of[0], (SEQ, D), 0.5, 4.0, ((0, 256),))
    queries = draw_queries(jax.random.fold_in(key_of[11], 71), 0)
    keys = draw_keys(jax.random.fold_in(key_of[11], 71), 0)
    values = gaussian(key_of[3], (SEQ, HEADS * HEAD_DIM), 1.0, 6.0, ((0, 8), (1, 32)))
    w_out = gaussian(key_of[4], (HEADS * HEAD_DIM, D), HEAD_DIM ** -0.5, 0.5, ((0, 32),))
    norm_gain = jnp.clip(1.0 + 0.15 * jax.random.normal(key_of[5], (D,), jnp.float32), 0.25, 1.75)
    expert_ids_keys = jax.random.split(jax.random.fold_in(key_of[6], 1), SEQ // TOK_DEV)
    expert_ids_turns = jax.random.permutation(jax.random.fold_in(key_of[6], 3), SEQ // TOK_DEV)
    expert_ids = jax.vmap(lambda own, number: assign_block(jax.random.fold_in(key_of[6], 2), own, number, TOK_DEV, EXPERTS, TOPK, CAP, 2))(expert_ids_keys, expert_ids_turns).reshape((SEQ, TOPK))
    gates = jnp.clip(0.1 + 0.9 * jax.random.uniform(key_of[7], (SEQ, TOPK), jnp.float32) ** block_scale(key_of[7], (SEQ, TOPK), ((0, 256),), -0.2, 0.2), 0.1, 1.0)
    w_gate = gaussian(key_of[8], (N_CTX, N_EXP, FF_EXP // PIECES, D), D ** -0.5, 0.09375, ((0, 8), (1, 32)))
    w_up = gaussian(key_of[9], (N_CTX, N_EXP, FF_EXP // PIECES, D), D ** -0.5, 0.09375, ((0, 8), (1, 32)))
    w_down = gaussian(key_of[10], (N_CTX, N_EXP, FF_EXP // PIECES, D), FF_EXP ** -0.5, 0.15625, ((0, 8), (1, 32)))
    return {"stream_in": stream_in, "queries": queries, "keys": keys, "values": values, "w_out": w_out, "norm_gain": norm_gain, "expert_ids": expert_ids, "gates": gates, "w_gate": w_gate, "w_up": w_up, "w_down": w_down}


masked_score = -1e+30

def partial_attention(query_block, query_start, key_block, value_block, key_start):
    scale = query_block.shape[1] ** (-0.5)
    scores = lax.dot_general(query_block, key_block, (((1,), (1,)), ((), ())), preferred_element_type=jnp.float32) * scale
    query_pos = query_start + jnp.arange(query_block.shape[0], dtype=jnp.int32)
    key_pos = key_start + jnp.arange(key_block.shape[0], dtype=jnp.int32)
    visible = key_pos[None, :] <= query_pos[:, None]
    scores = jnp.where(visible, scores, masked_score)
    valid = jnp.any(visible, axis=1)
    top = jnp.where(valid, lax.optimization_barrier(jnp.max(scores, axis=1)), 0.0)
    weights = jnp.where(visible, jnp.exp(scores - top[:, None]), 0.0)
    total = jnp.where(valid, lax.optimization_barrier(jnp.sum(weights, axis=1)), 1.0)
    probs = (weights / total[:, None]).astype(jnp.bfloat16)
    partial_out = jnp.dot(probs, value_block, preferred_element_type=jnp.float32)
    log_total = jnp.where(valid, top + jnp.log(total), masked_score)
    return (partial_out, log_total)

def merge_partials(outs, log_totals):
    top = lax.optimization_barrier(jnp.max(log_totals, axis=0))
    scaled = jnp.exp(log_totals - top[None, :])
    share = scaled / lax.optimization_barrier(jnp.sum(scaled, axis=0))[None, :]
    return lax.optimization_barrier(jnp.sum(outs * share[:, :, None], axis=0)).astype(jnp.bfloat16)

def reference(stream_in, queries, keys, values, w_out, norm_gain, expert_ids, gates, w_gate, w_up, w_down):
    head_count = queries.shape[1] // HEAD_DIM

    def one_head(projected, head):
        column_start = head * HEAD_DIM
        query_head = lax.dynamic_slice_in_dim(queries, column_start, HEAD_DIM, 1)
        key_head = lax.dynamic_slice_in_dim(keys, column_start, HEAD_DIM, 1)
        value_head = lax.dynamic_slice_in_dim(values, column_start, HEAD_DIM, 1)
        outs = []
        totals = []
        for shard_index in range(N_CTX):
            lower = shard_index * SHARD
            partial_value, part_total = partial_attention(query_head, 0, key_head[lower:lower + SHARD], value_head[lower:lower + SHARD], lower)
            outs.append(partial_value)
            totals.append(part_total)
        attended = merge_partials(jnp.stack(outs), jnp.stack(totals))
        out_rows = lax.dynamic_slice_in_dim(w_out, column_start, HEAD_DIM, 0)
        term = jnp.dot(attended, out_rows, preferred_element_type=jnp.float32).astype(jnp.bfloat16)
        term = lax.optimization_barrier(term)
        return (projected + term.astype(jnp.float32), None)
    projected, _ = lax.scan(one_head, jnp.zeros((SEQ, D), jnp.float32), jnp.arange(head_count, dtype=jnp.int32))
    hidden = stream_in.astype(jnp.float32) + projected
    normed = (hidden * lax.rsqrt(lax.optimization_barrier(jnp.mean(hidden * hidden, axis=1, keepdims=True)) + 1e-06) * norm_gain[None, :]).astype(jnp.bfloat16)
    flat_ids = expert_ids.reshape(-1).astype(jnp.int32)
    flat_gates = gates.reshape(-1)
    most_rows = CAP * N_CTX * N_EXP
    order = jnp.argsort(flat_ids, stable=True).astype(jnp.int32)
    padded = jnp.concatenate([order, jnp.zeros((most_rows,), jnp.int32)])

    def one_expert(combined, expert):
        start = jnp.sum(flat_ids < expert).astype(jnp.int32)
        count = jnp.sum(flat_ids == expert).astype(jnp.int32)
        picked = lax.dynamic_slice_in_dim(padded, start, most_rows, 0)
        living = jnp.arange(most_rows, dtype=jnp.int32) < count
        token_rows = picked // TOPK
        chosen = normed[token_rows]
        group = expert // N_EXP
        owner = expert % N_EXP
        total = jnp.zeros((most_rows, D), jnp.float32)
        for piece_index in range(PIECES):
            row = group * PIECES + piece_index
            gate_piece = w_gate[row, owner]
            up_piece = w_up[row, owner]
            down_piece = w_down[row, owner]
            gate_value = lax.dot_general(chosen, gate_piece, (((1,), (1,)), ((), ())), preferred_element_type=jnp.float32)
            up_value = lax.dot_general(chosen, up_piece, (((1,), (1,)), ((), ())), preferred_element_type=jnp.float32)
            activated = (jax.nn.silu(gate_value) * up_value).astype(jnp.bfloat16)
            down = jnp.dot(activated, down_piece, preferred_element_type=jnp.float32).astype(jnp.bfloat16)
            down = lax.optimization_barrier(down)
            total = total + down.astype(jnp.float32)
        routed = total.astype(jnp.bfloat16)
        weight = jnp.where(living, flat_gates[picked], 0.0)
        combined = combined.at[token_rows].add(weight[:, None] * routed.astype(jnp.float32))
        return (combined, None)
    combined, _ = lax.scan(one_expert, jnp.zeros((SEQ, D), jnp.float32), jnp.arange(EXPERTS, dtype=jnp.int32))
    return (hidden + combined).astype(jnp.bfloat16)
```

```python
import jax
import jax.numpy as jnp
from jax import lax
from jax.experimental import pallas as pl
from jax.experimental.pallas import tpu as pltpu
from jax.sharding import Mesh, PartitionSpec as P

CTX = ("xh", "y")
QUAD = ("xl", "core")
EXP = ("z", "xl", "core")
HOME = ("xh", "z", "xl", "core")

SUB = 16
LANE = 256

f32 = jnp.float32
bf16 = jnp.bfloat16
VMEM = pl.BlockSpec(memory_space=pltpu.VMEM)
SMEM = pl.BlockSpec(memory_space=pltpu.SMEM)


def swap_matrix(outer, inner):
    size = outer * inner
    row = lax.broadcasted_iota(jnp.int32, (size, size), 0)
    col = lax.broadcasted_iota(jnp.int32, (size, size), 1)
    return (col == (row % inner) * outer + row // inner).astype(bf16)


def attention_kernel(index, q_ref, kv_ref, out_ref):
    own = index[0]
    q = q_ref[...]
    head = q.shape[1]
    scale = head ** (-0.5)

    def scores_of(j):
        return (
            lax.dot_general(
                q, kv_ref[j, :, :head], (((1,), (1,)), ((), ())), preferred_element_type=f32
            )
            * scale
        )

    scores = scores_of(own)
    row = lax.broadcasted_iota(jnp.int32, scores.shape, 0)
    col = lax.broadcasted_iota(jnp.int32, scores.shape, 1)
    scores = jnp.where(col <= row, scores, -1e30)
    top = jnp.max(scores, axis=1, keepdims=True)
    weights = jnp.exp(scores - top)
    total = jnp.sum(weights, axis=1, keepdims=True)
    acc = jnp.dot(weights.astype(bf16), kv_ref[own, :, head:], preferred_element_type=f32)

    def step(j, carry):
        top, total, acc = carry
        scores = scores_of(j)
        higher = jnp.maximum(top, jnp.max(scores, axis=1, keepdims=True))
        fade = jnp.exp(top - higher)
        weights = jnp.exp(scores - higher)
        total = total * fade + jnp.sum(weights, axis=1, keepdims=True)
        acc = acc * fade + jnp.dot(
            weights.astype(bf16), kv_ref[j, :, head:], preferred_element_type=f32
        )
        return higher, total, acc

    top, total, acc = lax.fori_loop(0, own, step, (top, total, acc))
    out_ref[...] = (acc / total).astype(bf16)


def project_kernel(a0, a1, a2, a3, w0, w1, w2, w3, out_ref):
    acc = jnp.dot(a0[...], w0[...], preferred_element_type=f32)
    for a, w in ((a1, w1), (a2, w2), (a3, w3)):
        acc += jnp.dot(a[...], w[...], preferred_element_type=f32)
    out_ref[...] = acc.astype(bf16)


def dispatch_kernel(ids, proj, stream, gain, hidden, first, second, count, rows):
    tokens, width = stream.shape
    parts = proj.shape[0]
    part = width // parts
    squares = jnp.zeros((tokens, 1), f32)
    for p in range(parts):
        cols = slice(p * part, (p + 1) * part)
        h = stream[:, cols].astype(f32) + proj[p]
        hidden[:, cols] = h
        squares += jnp.sum(h * h, axis=1, keepdims=True)
    norm = lax.rsqrt(squares / width + 1e-06)
    blocks = []
    for k in range(SUB):
        cols = slice(k * LANE, (k + 1) * LANE)
        blocks.append(hidden[:, cols] * norm * gain[:, cols])
    normed = jnp.concatenate(blocks, axis=0).astype(bf16)
    swapped = jnp.dot(swap_matrix(tokens, SUB), normed, preferred_element_type=f32)
    rows[...] = swapped.astype(bf16).reshape(rows.shape)
    first[...] = jnp.zeros_like(first)
    second[...] = jnp.zeros_like(second)
    for e in range(first.shape[0]):
        count[e] = 0
    for t in range(tokens):
        for k in range(ids.shape[1]):
            e = ids[t, k]
            seen = count[e]
            count[e] = seen + 1

            @pl.when(seen == 0)
            def _():
                first[e] = rows[t]

            @pl.when(seen != 0)
            def _():
                second[e] = rows[t]


def expert_kernel(x0, x1, x2, x3, gate_ref, up_ref, down_ref, o0, o1, o2, o3, flat, mixed):
    swap = swap_matrix(SUB, SUB)
    per = x0.shape[0] // SUB
    for s, x in enumerate((x0, x1, x2, x3)):
        for b in range(per):
            block = x[b * SUB : (b + 1) * SUB].reshape(SUB * SUB, LANE)
            turned = jnp.dot(swap, block, preferred_element_type=f32).astype(bf16)
            at = (s * per + b) * SUB
            for k in range(SUB):
                flat[at : at + SUB, k * LANE : (k + 1) * LANE] = turned[k * SUB : (k + 1) * SUB]
    x = flat[...]
    gate = lax.dot_general(x, gate_ref[...], (((1,), (1,)), ((), ())), preferred_element_type=f32)
    up = lax.dot_general(x, up_ref[...], (((1,), (1,)), ((), ())), preferred_element_type=f32)
    activated = (gate / (1.0 + jnp.exp(-gate)) * up).astype(bf16)
    for k in range(SUB):
        down = jnp.dot(
            activated, down_ref[:, k * LANE : (k + 1) * LANE], preferred_element_type=f32
        ).astype(bf16)
        for g in range(4 * per):
            mixed[g, k * SUB : (k + 1) * SUB, :] = down[g * SUB : (g + 1) * SUB]
    for s, o in enumerate((o0, o1, o2, o3)):
        for b in range(per):
            turned = jnp.dot(swap, mixed[s * per + b], preferred_element_type=f32).astype(bf16)
            o[b * SUB : (b + 1) * SUB] = turned.reshape(SUB, SUB, LANE)


def combine_kernel(ids, gates, hidden, first, second, out_ref, count, total):
    tokens = hidden.shape[0]
    for e in range(first.shape[0]):
        count[e] = 0
    for t in range(tokens):
        acc = jnp.zeros((SUB, LANE), f32)
        for k in range(ids.shape[1]):
            e = ids[t, k]
            seen = count[e]
            count[e] = seen + 1
            routed = jnp.where(seen == 0, first[e].astype(f32), second[e].astype(f32))
            acc += gates[t, k] * routed
        for k in range(SUB):
            total[t : t + 1, k * LANE : (k + 1) * LANE] = acc[k : k + 1]
    out_ref[...] = (hidden[...] + total[...]).astype(bf16)


def shift(steps, count):
    return [(i, (i + steps) % count) for i in range(count)]


def flip(bits):
    return [(i, i ^ bits) for i in range(4)]


def on_device(
    stream_in, queries, keys, values, w_out, norm_gain, expert_ids, gates, w_gate, w_up, w_down
):
    shard, head = queries.shape
    tokens, width = stream_in.shape
    n_ctx = 8
    n_z = 8
    experts = 64
    quarter = width // 4
    place = lax.axis_index("xh") * 4 + lax.axis_index("y")
    quad = lax.axis_index(QUAD)

    weights = []
    for d in range(4):
        cols = lax.dynamic_slice_in_dim(w_out, (quad ^ d) * quarter, quarter, 1)
        weights.append(cols if d == 0 else lax.ppermute(cols, QUAD, flip(d)))

    both = jnp.concatenate([keys, values], axis=1)
    copies = jnp.broadcast_to(both[None], (n_ctx, shard, 2 * head))
    everyone = lax.all_to_all(copies, CTX, 0, 0, tiled=True)
    attended = pl.pallas_call(
        attention_kernel,
        out_shape=jax.ShapeDtypeStruct((shard, head), bf16),
        in_specs=[SMEM, VMEM, VMEM],
        out_specs=VMEM,
        name="attention",
    )(place.reshape(1).astype(jnp.int32), queries, everyone)

    heads = [attended] + [lax.ppermute(attended, QUAD, flip(d)) for d in (1, 2, 3)]
    term = pl.pallas_call(
        project_kernel,
        out_shape=jax.ShapeDtypeStruct((shard, quarter), bf16),
        in_specs=[VMEM] * 8,
        out_specs=VMEM,
        name="project",
    )(*heads, *weights)
    terms = lax.all_to_all(term.reshape(n_z, shard // n_z, quarter), "z", 0, 0, tiled=True)
    summed = jnp.sum(terms.astype(f32), axis=0)
    proj = lax.all_to_all(summed.reshape(4, tokens, quarter), QUAD, 0, 0, tiled=True)

    row_block = (experts, SUB, LANE)
    hidden, first, second = pl.pallas_call(
        dispatch_kernel,
        out_shape=(
            jax.ShapeDtypeStruct((tokens, width), f32),
            jax.ShapeDtypeStruct(row_block, bf16),
            jax.ShapeDtypeStruct(row_block, bf16),
        ),
        in_specs=[SMEM, VMEM, VMEM, VMEM],
        out_specs=(VMEM, VMEM, VMEM),
        scratch_shapes=[
            pltpu.SMEM((experts,), jnp.int32),
            pltpu.VMEM((tokens, SUB, LANE), bf16),
        ],
        name="dispatch",
    )(expert_ids, proj, stream_in, norm_gain.reshape(1, width))

    expert_call = pl.pallas_call(
        expert_kernel,
        out_shape=(jax.ShapeDtypeStruct(row_block, bf16),) * 4,
        in_specs=[VMEM] * 7,
        out_specs=(VMEM,) * 4,
        scratch_shapes=[
            pltpu.VMEM((4 * experts, width), bf16),
            pltpu.VMEM((4 * experts // SUB, SUB * SUB, LANE), bf16),
        ],
        compiler_params=pltpu.CompilerParams(vmem_limit_bytes=40 * 1024 * 1024),
        name="experts",
    )
    returned = []
    for rows in (first, second):
        own = lax.all_to_all(rows, HOME, 0, 0, tiled=True)
        others = [lax.ppermute(own, "y", shift(d, 4)) for d in (1, 2, 3)]
        outs = expert_call(own, *others, w_gate[0, 0], w_up[0, 0], w_down[0, 0])
        pieces = [outs[0]] + [lax.ppermute(outs[d], "y", shift(-d, 4)) for d in (1, 2, 3)]
        total = pieces[0].astype(f32)
        for piece in pieces[1:]:
            total = total + piece.astype(f32)
        returned.append(lax.all_to_all(total.astype(bf16), HOME, 0, 0, tiled=True))

    return pl.pallas_call(
        combine_kernel,
        out_shape=jax.ShapeDtypeStruct((tokens, width), bf16),
        in_specs=[SMEM, SMEM, VMEM, VMEM, VMEM],
        out_specs=VMEM,
        scratch_shapes=[pltpu.SMEM((experts,), jnp.int32), pltpu.VMEM((tokens, width), f32)],
        name="combine",
    )(expert_ids, gates, hidden, *returned)


def solution(mesh):
    fine = Mesh(mesh.devices.reshape(2, 4, 8, 2, 2), ("xh", "y", "z", "xl", "core"))
    token = CTX + EXP
    placed = (
        P(token, None),
        P(CTX, EXP),
        P(CTX, EXP),
        P(CTX, EXP),
        P(EXP, None),
        P(),
        P(token, None),
        P(token, None),
        P(CTX, EXP, None, None),
        P(CTX, EXP, None, None),
        P(CTX, EXP, None, None),
    )
    return jax.shard_map(
        on_device, mesh=fine, in_specs=placed, out_specs=P(token, None), check_vma=False
    )
```

```python
import functools

import jax
import jax.numpy as jnp
from jax import lax
from jax.experimental import pallas as pl
from jax.experimental.pallas import tpu as pltpu
from jax.sharding import Mesh, PartitionSpec as P

CTX = ("xh", "y")
QUAD = ("xl", "core")
EXP = ("z", "xl", "core")
HOME = ("xh", "z", "xl", "core")

SUB = 16
LANE = 256

f32 = jnp.float32
bf16 = jnp.bfloat16
VMEM = pl.BlockSpec(memory_space=pltpu.VMEM)
SMEM = pl.BlockSpec(memory_space=pltpu.SMEM)
ANY = pl.BlockSpec(memory_space=pl.ANY)


def swap_matrix(outer, inner):
    size = outer * inner
    row = lax.broadcasted_iota(jnp.int32, (size, size), 0)
    col = lax.broadcasted_iota(jnp.int32, (size, size), 1)
    return (col == (row % inner) * outer + row // inner).astype(bf16)


def pack_kernel(keys, values, out_at, both, sent):
    head = keys.shape[1]
    both[:, :head] = keys[...]
    both[:, head:] = values[...]
    copies = [
        pltpu.make_async_copy(both, out_at.at[j], sent.at[j]) for j in range(out_at.shape[0])
    ]
    for copy in copies:
        copy.start()
    for copy in copies:
        copy.wait()


def attention_kernel(index, q_ref, kv_at, out_ref, kv_ref, arrived):
    own = index[0]

    def load(j):
        return pltpu.make_async_copy(kv_at.at[j], kv_ref.at[j], arrived.at[j])

    load(own).start()
    for j in range(kv_ref.shape[0]):

        @pl.when(j < own)
        def _():
            load(j).start()

    load(own).wait()
    q = q_ref[...]
    head = q.shape[1]
    scale = head ** (-0.5)

    def scores_of(j):
        return (
            lax.dot_general(
                q, kv_ref[j, :, :head], (((1,), (1,)), ((), ())), preferred_element_type=f32
            )
            * scale
        )

    scores = scores_of(own)
    row = lax.broadcasted_iota(jnp.int32, scores.shape, 0)
    col = lax.broadcasted_iota(jnp.int32, scores.shape, 1)
    scores = jnp.where(col <= row, scores, -1e30)
    top = jnp.max(scores, axis=1, keepdims=True)
    weights = jnp.exp(scores - top)
    total = jnp.sum(weights, axis=1, keepdims=True)
    acc = jnp.dot(weights.astype(bf16), kv_ref[own, :, head:], preferred_element_type=f32)

    def step(pair, carry):
        top, total, acc = carry
        blocks = (2 * pair, 2 * pair + 1)
        for j in blocks:

            @pl.when(j < own)
            def _():
                load(j).wait()

        scores = [jnp.where(j < own, scores_of(j), -1e30) for j in blocks]
        higher = jnp.maximum(top, jnp.max(jnp.maximum(*scores), axis=1, keepdims=True))
        fade = jnp.exp(top - higher)
        weights = [jnp.exp(part - higher) for part in scores]
        total = total * fade + jnp.sum(weights[0] + weights[1], axis=1, keepdims=True)
        acc = acc * fade
        for j, part in zip(blocks, weights):
            acc += jnp.dot(part.astype(bf16), kv_ref[j, :, head:], preferred_element_type=f32)
        return higher, total, acc

    top, total, acc = lax.fori_loop(0, (own + 1) // 2, step, (top, total, acc))
    out_ref[...] = (acc / total).astype(bf16)


def project_kernel(a0, a1, a2, a3, w0, w1, w2, w3, out_ref):
    heads = jnp.concatenate([a[...] for a in (a0, a1, a2, a3)], axis=1)
    weights = jnp.concatenate([w[...] for w in (w0, w1, w2, w3)], axis=0)
    out_ref[...] = jnp.dot(heads, weights, preferred_element_type=f32).astype(bf16)


def dispatch_kernel(ids, terms, stream, gain, hidden, outgoing, count, rows):
    tokens, width = stream.shape
    part = terms.shape[2]
    parts = width // part
    squares = jnp.zeros((tokens, 1), f32)
    for p in range(parts):
        cols = slice(p * part, (p + 1) * part)
        h = terms[p].astype(f32)
        for source in range(p + parts, terms.shape[0], parts):
            h += terms[source].astype(f32)
        h += stream[:, cols].astype(f32)
        hidden[:, cols] = h
        squares += jnp.sum(h * h, axis=1, keepdims=True)
    norm = lax.rsqrt(squares / width + 1e-06)
    blocks = []
    for k in range(SUB):
        cols = slice(k * LANE, (k + 1) * LANE)
        blocks.append(hidden[:, cols] * norm * gain[:, cols])
    normed = jnp.concatenate(blocks, axis=0).astype(bf16)
    swapped = jnp.dot(swap_matrix(tokens, SUB), normed, preferred_element_type=f32)
    rows[...] = swapped.astype(bf16).reshape(rows.shape)
    outgoing[...] = jnp.zeros_like(outgoing)
    for e in range(outgoing.shape[0] // 2):
        count[e] = 0
    for t in range(tokens):
        for k in range(ids.shape[1]):
            e = ids[t, k]
            seen = count[e]
            count[e] = seen + 1
            outgoing[2 * e + seen] = rows[t]


def expert_kernel(sizes_in, sizes_out, *refs):
    n_in, n_out = len(sizes_in), len(sizes_out)
    inputs, refs = refs[:n_in], refs[n_in:]
    stored, refs = refs[:3], refs[3:]
    outputs, refs = refs[:n_out], refs[n_out:]
    rows, gate_ref, up_ref, down_ref, flat, mixed, results, in_sem, weight_sem, out_sem = refs
    loads, at = [], 0
    for i, (source, size) in enumerate(zip(inputs, sizes_in)):
        loads.append(pltpu.make_async_copy(source, rows.at[at : at + size], in_sem.at[i]))
        loads[i].start()
        at += size
    weights = []
    for i, (source, target) in enumerate(zip(stored, (gate_ref, up_ref, down_ref))):
        weights.append(pltpu.make_async_copy(source, target, weight_sem.at[i]))
        weights[i].start()
    swap = swap_matrix(SUB, SUB)
    at = 0
    for load, size in zip(loads, sizes_in):
        load.wait()
        for start in range(at, at + size, SUB):
            block = rows[start : start + SUB].reshape(SUB * SUB, LANE)
            turned = jnp.dot(swap, block, preferred_element_type=f32).astype(bf16)
            for k in range(SUB):
                flat[start : start + SUB, k * LANE : (k + 1) * LANE] = turned[k * SUB : (k + 1) * SUB]
        at += size
    x = flat[...]
    weights[0].wait()
    gate = lax.dot_general(x, gate_ref[...], (((1,), (1,)), ((), ())), preferred_element_type=f32)
    weights[1].wait()
    up = lax.dot_general(x, up_ref[...], (((1,), (1,)), ((), ())), preferred_element_type=f32)
    activated = (gate / (1.0 + jnp.exp(-gate)) * up).astype(bf16)
    weights[2].wait()
    for k in range(SUB):
        down = jnp.dot(
            activated, down_ref[:, k * LANE : (k + 1) * LANE], preferred_element_type=f32
        ).astype(bf16)
        for g in range(at // SUB):
            mixed[g, k * SUB : (k + 1) * SUB, :] = down[g * SUB : (g + 1) * SUB]
    stores, at = [], 0
    for i, (target, size) in enumerate(zip(outputs, sizes_out)):
        for start in range(at, at + size, SUB):
            turned = jnp.dot(swap, mixed[start // SUB], preferred_element_type=f32).astype(bf16)
            results[start : start + SUB] = turned.reshape(SUB, SUB, LANE)
        stores.append(pltpu.make_async_copy(results.at[at : at + size], target, out_sem.at[i]))
        stores[i].start()
        at += size
    for store in stores:
        store.wait()


def total_kernel(*refs):
    pieces, out_ref = refs[:-1], refs[-1]
    each = len(pieces) // 2
    for slot in range(2):
        total = pieces[slot * each][...].astype(f32)
        for piece in pieces[slot * each + 1 : (slot + 1) * each]:
            total += piece[...].astype(f32)
        out_ref[:, slot * SUB : (slot + 1) * SUB] = total.astype(bf16)


def combine_kernel(ids, gates, hidden, routed, out_ref, count, total):
    tokens = hidden.shape[0]
    for e in range(routed.shape[0]):
        count[e] = 0
    for t in range(tokens):
        acc = jnp.zeros((SUB, LANE), f32)
        for k in range(ids.shape[1]):
            e = ids[t, k]
            seen = count[e]
            count[e] = seen + 1
            acc += gates[t, k] * routed[e, pl.ds(pl.multiple_of(seen * SUB, SUB), SUB)].astype(f32)
        for k in range(SUB):
            total[t : t + 1, k * LANE : (k + 1) * LANE] = acc[k : k + 1]
    out_ref[...] = (hidden[...] + total[...]).astype(bf16)


def shift(steps, count):
    return [(i, (i + steps) % count) for i in range(count)]


def flip(bits):
    return [(i, i ^ bits) for i in range(4)]


def on_device(
    stream_in, queries, keys, values, w_out, norm_gain, expert_ids, gates, w_gate, w_up, w_down
):
    shard, head = queries.shape
    tokens, width = stream_in.shape
    n_ctx = 8
    experts = 64
    hidden_units = w_gate.shape[2]
    quarter = width // 4
    place = lax.axis_index("xh") * 4 + lax.axis_index("y")
    quad = lax.axis_index(QUAD)

    weights = []
    for d in range(4):
        cols = lax.dynamic_slice_in_dim(w_out, (quad ^ d) * quarter, quarter, 1)
        weights.append(cols if d == 0 else lax.ppermute(cols, QUAD, flip(d)))

    copies = pl.pallas_call(
        pack_kernel,
        out_shape=jax.ShapeDtypeStruct((n_ctx, shard, 2 * head), bf16),
        in_specs=[VMEM, VMEM],
        out_specs=ANY,
        scratch_shapes=[pltpu.VMEM((shard, 2 * head), bf16), pltpu.SemaphoreType.DMA((n_ctx,))],
        name="pack",
    )(keys, values)
    everyone = lax.all_to_all(copies, CTX, 0, 0, tiled=True)
    attended = pl.pallas_call(
        attention_kernel,
        out_shape=jax.ShapeDtypeStruct((shard, head), bf16),
        in_specs=[SMEM, VMEM, ANY],
        out_specs=VMEM,
        scratch_shapes=[
            pltpu.VMEM((n_ctx, shard, 2 * head), bf16),
            pltpu.SemaphoreType.DMA((n_ctx,)),
        ],
        compiler_params=pltpu.CompilerParams(vmem_limit_bytes=8 * 1024 * 1024),
        name="attention",
    )(place.reshape(1).astype(jnp.int32), queries, everyone)

    heads = [attended] + [lax.ppermute(attended, QUAD, flip(d)) for d in (1, 2, 3)]
    term = pl.pallas_call(
        project_kernel,
        out_shape=jax.ShapeDtypeStruct((shard, quarter), bf16),
        in_specs=[VMEM] * 8,
        out_specs=VMEM,
        name="project",
    )(*heads, *weights)
    terms = lax.all_to_all(term.reshape(-1, tokens, quarter), EXP, 0, 0, tiled=True)

    slots = 2 * experts
    hidden, outgoing = pl.pallas_call(
        dispatch_kernel,
        out_shape=(
            jax.ShapeDtypeStruct((tokens, width), f32),
            jax.ShapeDtypeStruct((slots, SUB, LANE), bf16),
        ),
        in_specs=[SMEM, VMEM, VMEM, VMEM],
        out_specs=(VMEM, VMEM),
        scratch_shapes=[
            pltpu.SMEM((experts,), jnp.int32),
            pltpu.VMEM((tokens, SUB, LANE), bf16),
        ],
        name="dispatch",
    )(expert_ids, terms, stream_in, norm_gain.reshape(1, width))

    def home(rows):
        return lax.all_to_all(rows, HOME, 0, 0, tiled=True)

    def block(rows):
        return jax.ShapeDtypeStruct((rows, SUB, LANE), bf16)

    per = experts
    def expert_call(sizes_out, *inputs):
        sizes_in = tuple(x.shape[0] for x in inputs)
        total = sum(sizes_in)
        weight = pltpu.VMEM((hidden_units, width), bf16)
        return pl.pallas_call(
            functools.partial(expert_kernel, sizes_in, sizes_out),
            out_shape=tuple(block(size) for size in sizes_out),
            in_specs=[ANY] * (len(inputs) + 3),
            out_specs=(ANY,) * len(sizes_out),
            scratch_shapes=[
                pltpu.VMEM((total, SUB, LANE), bf16),
                weight,
                weight,
                weight,
                pltpu.VMEM((total, width), bf16),
                pltpu.VMEM((total // SUB, SUB * SUB, LANE), bf16),
                pltpu.VMEM((total, SUB, LANE), bf16),
                pltpu.SemaphoreType.DMA((len(sizes_in),)),
                pltpu.SemaphoreType.DMA((3,)),
                pltpu.SemaphoreType.DMA((len(sizes_out),)),
            ],
            compiler_params=pltpu.CompilerParams(vmem_limit_bytes=62 * 1024 * 1024),
            cost_estimate=pl.CostEstimate(
                flops=6 * total * hidden_units * width,
                bytes_accessed=6 * hidden_units * width,
                transcendentals=0,
            ),
            name="experts",
        )(*inputs, w_gate[0, 0], w_up[0, 0], w_down[0, 0])

    def up(rows):
        return lax.ppermute(rows, "y", shift(1, 4))

    def down(rows):
        return lax.ppermute(rows, "y", shift(-1, 4))

    def across(rows):
        return lax.ppermute(rows, "y", shift(2, 4))

    arrived = home(outgoing.reshape(experts, 2 * SUB, LANE))
    rows_a, rows_b = arrived[:, :SUB], arrived[:, SUB:]
    near = (up(rows_a), up(rows_b), down(rows_a), down(rows_b))
    own = expert_call((per, per), rows_a, rows_b)
    (below_a, below_b, above_a, above_b), own = lax.optimization_barrier((near, own))
    far = (down(above_a), up(below_b))
    early = expert_call((per,) * 4, below_a, above_a, below_b, above_b)
    early, far = lax.optimization_barrier((early, far))
    near_a = (down(early[0]), up(early[1]))
    late = expert_call((per, per), *far)
    near_a, late = lax.optimization_barrier((near_a, late))
    pieces = (own[0], *near_a, across(late[0]))
    pieces += (own[1], down(early[2]), up(early[3]), across(late[1]))
    part = experts // 4
    totals = pl.pallas_call(
        total_kernel,
        grid=(4,),
        out_shape=jax.ShapeDtypeStruct((experts, 2 * SUB, LANE), bf16),
        in_specs=[pl.BlockSpec((part, SUB, LANE), lambda i: (i, 0, 0))] * len(pieces),
        out_specs=pl.BlockSpec((part, 2 * SUB, LANE), lambda i: (i, 0, 0)),
        name="totals",
    )(*pieces)
    returned = home(totals)

    return pl.pallas_call(
        combine_kernel,
        out_shape=jax.ShapeDtypeStruct((tokens, width), bf16),
        in_specs=[SMEM, SMEM, VMEM, VMEM],
        out_specs=VMEM,
        scratch_shapes=[pltpu.SMEM((experts,), jnp.int32), pltpu.VMEM((tokens, width), f32)],
        name="combine",
    )(expert_ids, gates, hidden, returned)


def solution(mesh):
    fine = Mesh(mesh.devices.reshape(2, 4, 8, 2, 2), ("xh", "y", "z", "xl", "core"))
    token = CTX + EXP
    placed = (
        P(token, None),
        P(CTX, EXP),
        P(CTX, EXP),
        P(CTX, EXP),
        P(EXP, None),
        P(),
        P(token, None),
        P(token, None),
        P(CTX, EXP, None, None),
        P(CTX, EXP, None, None),
        P(CTX, EXP, None, None),
    )
    return jax.shard_map(
        on_device, mesh=fine, in_specs=placed, out_specs=P(token, None), check_vma=False
    )
```

```python
import functools

import jax
import jax.numpy as jnp
from jax import lax
from jax.experimental import pallas as pl
from jax.experimental.pallas import tpu as pltpu
from jax.sharding import Mesh, PartitionSpec as P

CTX = ("xh", "y")
QUAD = ("xl", "core")
EXP = ("z", "xl", "core")
HOME = ("xh", "z", "xl", "core")

SUB = 16
LANE = 256

f32 = jnp.float32
bf16 = jnp.bfloat16
VMEM = pl.BlockSpec(memory_space=pltpu.VMEM)
SMEM = pl.BlockSpec(memory_space=pltpu.SMEM)
ANY = pl.BlockSpec(memory_space=pl.ANY)


def swap_matrix(outer, inner):
    size = outer * inner
    row = lax.broadcasted_iota(jnp.int32, (size, size), 0)
    col = lax.broadcasted_iota(jnp.int32, (size, size), 1)
    return (col == (row % inner) * outer + row // inner).astype(bf16)


def pack_kernel(keys, values, out_at, both, sent):
    head = keys.shape[1]
    both[:, :head] = keys[...]
    both[:, head:] = values[...]
    copies = [
        pltpu.make_async_copy(both, out_at.at[j], sent.at[j]) for j in range(out_at.shape[0])
    ]
    for copy in copies:
        copy.start()
    for copy in copies:
        copy.wait()


def attention_kernel(index, q_ref, kv_at, out_ref, kv_ref, arrived):
    own = index[0]

    def load(j):
        return pltpu.make_async_copy(kv_at.at[j], kv_ref.at[j], arrived.at[j])

    load(own).start()
    for j in range(kv_ref.shape[0]):

        @pl.when(j < own)
        def _():
            load(j).start()

    load(own).wait()
    q = q_ref[...]
    head = q.shape[1]
    scale = head ** (-0.5)

    def scores_of(j):
        return (
            lax.dot_general(
                q, kv_ref[j, :, :head], (((1,), (1,)), ((), ())), preferred_element_type=f32
            )
            * scale
        )

    scores = scores_of(own)
    row = lax.broadcasted_iota(jnp.int32, scores.shape, 0)
    col = lax.broadcasted_iota(jnp.int32, scores.shape, 1)
    scores = jnp.where(col <= row, scores, -1e30)
    top = jnp.max(scores, axis=1, keepdims=True)
    weights = jnp.exp(scores - top)
    total = jnp.sum(weights, axis=1, keepdims=True)
    acc = jnp.dot(weights.astype(bf16), kv_ref[own, :, head:], preferred_element_type=f32)

    def step(pair, carry):
        top, total, acc = carry
        blocks = (2 * pair, 2 * pair + 1)
        for j in blocks:

            @pl.when(j < own)
            def _():
                load(j).wait()

        scores = [jnp.where(j < own, scores_of(j), -1e30) for j in blocks]
        higher = jnp.maximum(top, jnp.max(jnp.maximum(*scores), axis=1, keepdims=True))
        fade = jnp.exp(top - higher)
        weights = [jnp.exp(part - higher) for part in scores]
        total = total * fade + jnp.sum(weights[0] + weights[1], axis=1, keepdims=True)
        acc = acc * fade
        for j, part in zip(blocks, weights):
            acc += jnp.dot(part.astype(bf16), kv_ref[j, :, head:], preferred_element_type=f32)
        return higher, total, acc

    top, total, acc = lax.fori_loop(0, (own + 1) // 2, step, (top, total, acc))
    out_ref[...] = (acc / total).astype(bf16)


def project_kernel(a0, a1, a2, a3, w0, w1, w2, w3, out_ref):
    heads = jnp.concatenate([a[...] for a in (a0, a1, a2, a3)], axis=1)
    weights = jnp.concatenate([w[...] for w in (w0, w1, w2, w3)], axis=0)
    out_ref[...] = jnp.dot(heads, weights, preferred_element_type=f32).astype(bf16)


def dispatch_kernel(ids, terms, stream, gain, hidden, outgoing, count, rows):
    tokens, width = stream.shape
    part = terms.shape[2]
    parts = width // part
    squares = jnp.zeros((tokens, 1), f32)
    for p in range(parts):
        cols = slice(p * part, (p + 1) * part)
        h = terms[p].astype(f32)
        for source in range(p + parts, terms.shape[0], parts):
            h += terms[source].astype(f32)
        h += stream[:, cols].astype(f32)
        hidden[:, cols] = h
        squares += jnp.sum(h * h, axis=1, keepdims=True)
    norm = lax.rsqrt(squares / width + 1e-06)
    blocks = []
    for k in range(SUB):
        cols = slice(k * LANE, (k + 1) * LANE)
        blocks.append(hidden[:, cols] * norm * gain[:, cols])
    normed = jnp.concatenate(blocks, axis=0).astype(bf16)
    swapped = jnp.dot(swap_matrix(tokens, SUB), normed, preferred_element_type=f32)
    rows[...] = swapped.astype(bf16).reshape(rows.shape)
    outgoing[...] = jnp.zeros_like(outgoing)
    for e in range(outgoing.shape[0] // 2):
        count[e] = 0
    for t in range(tokens):
        for k in range(ids.shape[1]):
            e = ids[t, k]
            seen = count[e]
            count[e] = seen + 1
            outgoing[2 * e + seen] = rows[t]


def expert_kernel(sizes_in, sizes_out, *refs):
    n_in, n_out = len(sizes_in), len(sizes_out)
    inputs, refs = refs[:n_in], refs[n_in:]
    stored, refs = refs[:3], refs[3:]
    outputs, refs = refs[:n_out], refs[n_out:]
    rows, gate_ref, up_ref, down_ref, flat, mixed, results, in_sem, weight_sem, out_sem = refs
    loads, at = [], 0
    for i, (source, size) in enumerate(zip(inputs, sizes_in)):
        loads.append(pltpu.make_async_copy(source, rows.at[at : at + size], in_sem.at[i]))
        loads[i].start()
        at += size
    weights = []
    for i, (source, target) in enumerate(zip(stored, (gate_ref, up_ref, down_ref))):
        weights.append(pltpu.make_async_copy(source, target, weight_sem.at[i]))
        weights[i].start()
    swap = swap_matrix(SUB, SUB)
    at = 0
    for load, size in zip(loads, sizes_in):
        load.wait()
        for start in range(at, at + size, SUB):
            block = rows[start : start + SUB].reshape(SUB * SUB, LANE)
            turned = jnp.dot(swap, block, preferred_element_type=f32).astype(bf16)
            for k in range(SUB):
                flat[start : start + SUB, k * LANE : (k + 1) * LANE] = turned[k * SUB : (k + 1) * SUB]
        at += size
    x = flat[...]
    weights[0].wait()
    gate = lax.dot_general(x, gate_ref[...], (((1,), (1,)), ((), ())), preferred_element_type=f32)
    weights[1].wait()
    up = lax.dot_general(x, up_ref[...], (((1,), (1,)), ((), ())), preferred_element_type=f32)
    activated = (gate / (1.0 + jnp.exp(-gate)) * up).astype(bf16)
    weights[2].wait()
    for k in range(SUB):
        down = jnp.dot(
            activated, down_ref[:, k * LANE : (k + 1) * LANE], preferred_element_type=f32
        ).astype(bf16)
        for g in range(at // SUB):
            mixed[g, k * SUB : (k + 1) * SUB, :] = down[g * SUB : (g + 1) * SUB]
    stores, at = [], 0
    for i, (target, size) in enumerate(zip(outputs, sizes_out)):
        for start in range(at, at + size, SUB):
            turned = jnp.dot(swap, mixed[start // SUB], preferred_element_type=f32).astype(bf16)
            results[start : start + SUB] = turned.reshape(SUB, SUB, LANE)
        stores.append(pltpu.make_async_copy(results.at[at : at + size], target, out_sem.at[i]))
        stores[i].start()
        at += size
    for store in stores:
        store.wait()


def relay_kernel(below, from_above, above, from_below, out_below, out_above):
    out_below[...] = (below[...].astype(f32) + from_above[...].astype(f32)).astype(bf16)
    out_above[...] = (above[...].astype(f32) + from_below[...].astype(f32)).astype(bf16)


def total_kernel(a0, a1, a2, b0, b1, b2, out_ref):
    for half, pieces in enumerate(((a0, a1, a2), (b0, b1, b2))):
        total = pieces[0][...].astype(f32) + pieces[1][...].astype(f32)
        out_ref[half] = (total + pieces[2][...].astype(f32)).astype(bf16)


def combine_kernel(ids, gates, hidden, routed, out_ref, count, total):
    tokens = hidden.shape[0]
    for e in range(routed.shape[0]):
        count[e] = 0
    for t in range(tokens):
        acc = jnp.zeros((SUB, LANE), f32)
        for k in range(ids.shape[1]):
            e = ids[t, k]
            seen = count[e]
            count[e] = seen + 1
            acc += gates[t, k] * routed[e, pl.ds(pl.multiple_of(seen * SUB, SUB), SUB)].astype(f32)
        for k in range(SUB):
            total[t : t + 1, k * LANE : (k + 1) * LANE] = acc[k : k + 1]
    out_ref[...] = (hidden[...] + total[...]).astype(bf16)


def shift(steps, count):
    return [(i, (i + steps) % count) for i in range(count)]


def flip(bits):
    return [(i, i ^ bits) for i in range(4)]


def on_device(
    stream_in, queries, keys, values, w_out, norm_gain, expert_ids, gates, w_gate, w_up, w_down
):
    shard, head = queries.shape
    tokens, width = stream_in.shape
    n_ctx = 8
    experts = 64
    hidden_units = w_gate.shape[2]
    quarter = width // 4
    place = lax.axis_index("xh") * 4 + lax.axis_index("y")
    quad = lax.axis_index(QUAD)

    weights = []
    for d in range(4):
        cols = lax.dynamic_slice_in_dim(w_out, (quad ^ d) * quarter, quarter, 1)
        weights.append(cols if d == 0 else lax.ppermute(cols, QUAD, flip(d)))

    copies = pl.pallas_call(
        pack_kernel,
        out_shape=jax.ShapeDtypeStruct((n_ctx, shard, 2 * head), bf16),
        in_specs=[VMEM, VMEM],
        out_specs=ANY,
        scratch_shapes=[pltpu.VMEM((shard, 2 * head), bf16), pltpu.SemaphoreType.DMA((n_ctx,))],
        name="pack",
    )(keys, values)
    everyone = lax.all_to_all(copies, CTX, 0, 0, tiled=True)
    attended = pl.pallas_call(
        attention_kernel,
        out_shape=jax.ShapeDtypeStruct((shard, head), bf16),
        in_specs=[SMEM, VMEM, ANY],
        out_specs=VMEM,
        scratch_shapes=[
            pltpu.VMEM((n_ctx, shard, 2 * head), bf16),
            pltpu.SemaphoreType.DMA((n_ctx,)),
        ],
        compiler_params=pltpu.CompilerParams(vmem_limit_bytes=8 * 1024 * 1024),
        name="attention",
    )(place.reshape(1).astype(jnp.int32), queries, everyone)

    heads = [attended] + [lax.ppermute(attended, QUAD, flip(d)) for d in (1, 2, 3)]
    term = pl.pallas_call(
        project_kernel,
        out_shape=jax.ShapeDtypeStruct((shard, quarter), bf16),
        in_specs=[VMEM] * 8,
        out_specs=VMEM,
        compiler_params=pltpu.CompilerParams(vmem_limit_bytes=8 * 1024 * 1024),
        name="project",
    )(*heads, *weights)
    terms = lax.all_to_all(term.reshape(-1, tokens, quarter), EXP, 0, 0, tiled=True)

    slots = 2 * experts
    hidden, outgoing = pl.pallas_call(
        dispatch_kernel,
        out_shape=(
            jax.ShapeDtypeStruct((tokens, width), f32),
            jax.ShapeDtypeStruct((slots, SUB, LANE), bf16),
        ),
        in_specs=[SMEM, VMEM, VMEM, VMEM],
        out_specs=(VMEM, VMEM),
        scratch_shapes=[
            pltpu.SMEM((experts,), jnp.int32),
            pltpu.VMEM((tokens, SUB, LANE), bf16),
        ],
        compiler_params=pltpu.CompilerParams(vmem_limit_bytes=8 * 1024 * 1024),
        name="dispatch",
    )(expert_ids, terms, stream_in, norm_gain.reshape(1, width))

    def home(rows):
        return lax.all_to_all(rows, HOME, 0, 0, tiled=True)

    def block(rows):
        return jax.ShapeDtypeStruct((rows, SUB, LANE), bf16)

    per = experts
    def expert_call(sizes_out, *inputs):
        sizes_in = tuple(x.shape[0] for x in inputs)
        total = sum(sizes_in)
        weight = pltpu.VMEM((hidden_units, width), bf16)
        return pl.pallas_call(
            functools.partial(expert_kernel, sizes_in, sizes_out),
            out_shape=tuple(block(size) for size in sizes_out),
            in_specs=[ANY] * (len(inputs) + 3),
            out_specs=(ANY,) * len(sizes_out),
            scratch_shapes=[
                pltpu.VMEM((total, SUB, LANE), bf16),
                weight,
                weight,
                weight,
                pltpu.VMEM((total, width), bf16),
                pltpu.VMEM((total // SUB, SUB * SUB, LANE), bf16),
                pltpu.VMEM((total, SUB, LANE), bf16),
                pltpu.SemaphoreType.DMA((len(sizes_in),)),
                pltpu.SemaphoreType.DMA((3,)),
                pltpu.SemaphoreType.DMA((len(sizes_out),)),
            ],
            compiler_params=pltpu.CompilerParams(vmem_limit_bytes=62 * 1024 * 1024),
            cost_estimate=pl.CostEstimate(
                flops=6 * total * hidden_units * width,
                bytes_accessed=6 * hidden_units * width,
                transcendentals=0,
            ),
            name="experts",
        )(*inputs, w_gate[0, 0], w_up[0, 0], w_down[0, 0])

    def up(rows):
        return lax.ppermute(rows, "y", shift(1, 4))

    def down(rows):
        return lax.ppermute(rows, "y", shift(-1, 4))

    arrived = home(outgoing.reshape(experts, 2 * SUB, LANE)).reshape(slots, SUB, LANE)
    head, tail = arrived[:per], arrived[per:]
    near = (up(head), down(tail), up(tail), down(head))
    (own,) = expert_call((slots,), arrived)
    (below_head, above_tail, below_tail, above_head), own = lax.optimization_barrier((near, own))
    far = (up(below_head), down(above_tail))
    early = expert_call((per,) * 4, below_head, below_tail, above_head, above_tail)
    early, far = lax.optimization_barrier((early, far))
    ready = (down(early[0]), up(early[3]))
    late = expert_call((per, per), *far)
    ready, late = lax.optimization_barrier((ready, late))
    sum_below, sum_above = pl.pallas_call(
        relay_kernel,
        out_shape=(block(per), block(per)),
        in_specs=[VMEM] * 4,
        out_specs=(VMEM, VMEM),
        compiler_params=pltpu.CompilerParams(vmem_limit_bytes=8 * 1024 * 1024),
        name="relay",
    )(early[1], down(late[1]), early[2], up(late[0]))
    rest = (down(sum_below), up(sum_above))
    part = per // 2

    def part_at(first):
        return pl.BlockSpec((part, SUB, LANE), lambda i: (i + first, 0, 0))

    totals = pl.pallas_call(
        total_kernel,
        grid=(2,),
        out_shape=jax.ShapeDtypeStruct((2, per, SUB, LANE), bf16),
        in_specs=[part_at(0)] * 3 + [part_at(2), part_at(0), part_at(0)],
        out_specs=pl.BlockSpec((2, part, SUB, LANE), lambda i: (0, i, 0, 0)),
        compiler_params=pltpu.CompilerParams(vmem_limit_bytes=12 * 1024 * 1024),
        name="totals",
    )(own, ready[0], rest[1], own, rest[0], ready[1])
    totals = totals.reshape(experts, 2 * SUB, LANE)
    returned = home(totals)

    return pl.pallas_call(
        combine_kernel,
        out_shape=jax.ShapeDtypeStruct((tokens, width), bf16),
        in_specs=[SMEM, SMEM, VMEM, VMEM],
        out_specs=VMEM,
        scratch_shapes=[pltpu.SMEM((experts,), jnp.int32), pltpu.VMEM((tokens, width), f32)],
        compiler_params=pltpu.CompilerParams(vmem_limit_bytes=8 * 1024 * 1024),
        name="combine",
    )(expert_ids, gates, hidden, returned)


def solution(mesh):
    fine = Mesh(mesh.devices.reshape(2, 4, 8, 2, 2), ("xh", "y", "z", "xl", "core"))
    token = CTX + EXP
    placed = (
        P(token, None),
        P(CTX, EXP),
        P(CTX, EXP),
        P(CTX, EXP),
        P(EXP, None),
        P(),
        P(token, None),
        P(token, None),
        P(CTX, EXP, None, None),
        P(CTX, EXP, None, None),
        P(CTX, EXP, None, None),
    )
    return jax.shard_map(
        on_device, mesh=fine, in_specs=placed, out_specs=P(token, None), check_vma=False
    )
```

```python
import functools

import jax
import jax.numpy as jnp
from jax import lax
from jax.experimental import pallas as pl
from jax.experimental.pallas import tpu as pltpu
from jax.sharding import Mesh, PartitionSpec as P

CTX = ("xh", "y")
QUAD = ("xl", "core")
EXP = ("z", "xl", "core")
HOME = ("xh", "z", "xl", "core")

SUB = 16
LANE = 256

f32 = jnp.float32
bf16 = jnp.bfloat16
VMEM = pl.BlockSpec(memory_space=pltpu.VMEM)
SMEM = pl.BlockSpec(memory_space=pltpu.SMEM)
ANY = pl.BlockSpec(memory_space=pl.ANY)


def swap_matrix(outer, inner):
    size = outer * inner
    row = lax.broadcasted_iota(jnp.int32, (size, size), 0)
    col = lax.broadcasted_iota(jnp.int32, (size, size), 1)
    return (col == (row % inner) * outer + row // inner).astype(bf16)


def pack_kernel(keys, values, out_at, both, sent):
    head = keys.shape[1]
    both[:, :head] = keys[...]
    both[:, head:] = values[...]
    copies = [
        pltpu.make_async_copy(both, out_at.at[j], sent.at[j]) for j in range(out_at.shape[0])
    ]
    for copy in copies:
        copy.start()
    for copy in copies:
        copy.wait()


def attention_kernel(index, q_ref, kv_at, out_ref, kv_ref, arrived):
    own = index[0]

    def load(j):
        return pltpu.make_async_copy(kv_at.at[j], kv_ref.at[j], arrived.at[j])

    load(own).start()
    for j in range(kv_ref.shape[0]):

        @pl.when(j < own)
        def _():
            load(j).start()

    load(own).wait()
    q = q_ref[...]
    head = q.shape[1]
    scale = head ** (-0.5)

    def scores_of(j):
        return (
            lax.dot_general(
                q, kv_ref[j, :, :head], (((1,), (1,)), ((), ())), preferred_element_type=f32
            )
            * scale
        )

    scores = scores_of(own)
    row = lax.broadcasted_iota(jnp.int32, scores.shape, 0)
    col = lax.broadcasted_iota(jnp.int32, scores.shape, 1)
    scores = jnp.where(col <= row, scores, -1e30)
    top = jnp.max(scores, axis=1, keepdims=True)
    weights = jnp.exp(scores - top)
    total = jnp.sum(weights, axis=1, keepdims=True)
    acc = jnp.dot(weights.astype(bf16), kv_ref[own, :, head:], preferred_element_type=f32)

    def step(pair, carry):
        top, total, acc = carry
        blocks = (2 * pair, 2 * pair + 1)
        for j in blocks:

            @pl.when(j < own)
            def _():
                load(j).wait()

        scores = [jnp.where(j < own, scores_of(j), -1e30) for j in blocks]
        higher = jnp.maximum(top, jnp.max(jnp.maximum(*scores), axis=1, keepdims=True))
        fade = jnp.exp(top - higher)
        weights = [jnp.exp(part - higher) for part in scores]
        total = total * fade + jnp.sum(weights[0] + weights[1], axis=1, keepdims=True)
        acc = acc * fade
        for j, part in zip(blocks, weights):
            acc += jnp.dot(part.astype(bf16), kv_ref[j, :, head:], preferred_element_type=f32)
        return higher, total, acc

    top, total, acc = lax.fori_loop(0, (own + 1) // 2, step, (top, total, acc))
    out_ref[...] = (acc / total).astype(bf16)


def project_kernel(a0, a1, a2, a3, w0, w1, w2, w3, out_ref):
    heads = jnp.concatenate([a[...] for a in (a0, a1, a2, a3)], axis=1)
    weights = jnp.concatenate([w[...] for w in (w0, w1, w2, w3)], axis=0)
    out_ref[...] = jnp.dot(heads, weights, preferred_element_type=f32).astype(bf16)


def dispatch_kernel(ids, terms, stream, gain, hidden, outgoing, count, rows):
    tokens, width = stream.shape
    part = terms.shape[2]
    parts = width // part
    squares = jnp.zeros((tokens, 1), f32)
    for p in range(parts):
        cols = slice(p * part, (p + 1) * part)
        h = terms[p].astype(f32)
        for source in range(p + parts, terms.shape[0], parts):
            h += terms[source].astype(f32)
        h += stream[:, cols].astype(f32)
        hidden[:, cols] = h
        squares += jnp.sum(h * h, axis=1, keepdims=True)
    norm = lax.rsqrt(squares / width + 1e-06)
    blocks = []
    for k in range(SUB):
        cols = slice(k * LANE, (k + 1) * LANE)
        blocks.append(hidden[:, cols] * norm * gain[:, cols])
    normed = jnp.concatenate(blocks, axis=0).astype(bf16)
    swapped = jnp.dot(swap_matrix(tokens, SUB), normed, preferred_element_type=f32)
    rows[...] = swapped.astype(bf16).reshape(rows.shape)
    outgoing[...] = jnp.zeros_like(outgoing)
    for e in range(outgoing.shape[0] // 2):
        count[e] = 0
    for t in range(tokens):
        for k in range(ids.shape[1]):
            e = ids[t, k]
            seen = count[e]
            count[e] = seen + 1
            outgoing[2 * e + seen] = rows[t]


def expert_kernel(sizes_in, sizes_out, *refs):
    n_in, n_out = len(sizes_in), len(sizes_out)
    inputs, refs = refs[:n_in], refs[n_in:]
    stored, refs = refs[:3], refs[3:]
    outputs, refs = refs[:n_out], refs[n_out:]
    rows, gate_ref, up_ref, down_ref, flat, mixed, results, in_sem, weight_sem, out_sem = refs
    loads, at = [], 0
    for i, (source, size) in enumerate(zip(inputs, sizes_in)):
        loads.append(pltpu.make_async_copy(source, rows.at[at : at + size], in_sem.at[i]))
        loads[i].start()
        at += size
    weights = []
    for i, (source, target) in enumerate(zip(stored, (gate_ref, up_ref, down_ref))):
        weights.append(pltpu.make_async_copy(source, target, weight_sem.at[i]))
        weights[i].start()
    swap = swap_matrix(SUB, SUB)
    at = 0
    for load, size in zip(loads, sizes_in):
        load.wait()
        for start in range(at, at + size, SUB):
            block = rows[start : start + SUB].reshape(SUB * SUB, LANE)
            turned = jnp.dot(swap, block, preferred_element_type=f32).astype(bf16)
            for k in range(SUB):
                flat[start : start + SUB, k * LANE : (k + 1) * LANE] = turned[k * SUB : (k + 1) * SUB]
        at += size
    x = flat[...]
    weights[0].wait()
    gate = lax.dot_general(x, gate_ref[...], (((1,), (1,)), ((), ())), preferred_element_type=f32)
    weights[1].wait()
    up = lax.dot_general(x, up_ref[...], (((1,), (1,)), ((), ())), preferred_element_type=f32)
    activated = (gate / (1.0 + jnp.exp(-gate)) * up).astype(bf16)
    weights[2].wait()
    for k in range(SUB):
        down = jnp.dot(
            activated, down_ref[:, k * LANE : (k + 1) * LANE], preferred_element_type=f32
        ).astype(bf16)
        for g in range(at // SUB):
            mixed[g, k * SUB : (k + 1) * SUB, :] = down[g * SUB : (g + 1) * SUB]
    stores, at = [], 0
    for i, (target, size) in enumerate(zip(outputs, sizes_out)):
        for start in range(at, at + size, SUB):
            turned = jnp.dot(swap, mixed[start // SUB], preferred_element_type=f32).astype(bf16)
            results[start : start + SUB] = turned.reshape(SUB, SUB, LANE)
        stores.append(pltpu.make_async_copy(results.at[at : at + size], target, out_sem.at[i]))
        stores[i].start()
        at += size
    for store in stores:
        store.wait()


def relay_kernel(below, from_above, above, from_below, out_below, out_above):
    out_below[...] = (below[...].astype(f32) + from_above[...].astype(f32)).astype(bf16)
    out_above[...] = (above[...].astype(f32) + from_below[...].astype(f32)).astype(bf16)


def total_kernel(a0, a1, a2, b0, b1, b2, out_ref):
    for half, pieces in enumerate(((a0, a1, a2), (b0, b1, b2))):
        total = pieces[0][...].astype(f32) + pieces[1][...].astype(f32)
        out_ref[half] = (total + pieces[2][...].astype(f32)).astype(bf16)


def combine_kernel(ids, gates, hidden, routed, out_ref, count, total):
    tokens = hidden.shape[0]
    for e in range(routed.shape[0]):
        count[e] = 0
    for t in range(tokens):
        acc = jnp.zeros((SUB, LANE), f32)
        for k in range(ids.shape[1]):
            e = ids[t, k]
            seen = count[e]
            count[e] = seen + 1
            acc += gates[t, k] * routed[e, pl.ds(pl.multiple_of(seen * SUB, SUB), SUB)].astype(f32)
        for k in range(SUB):
            total[t : t + 1, k * LANE : (k + 1) * LANE] = acc[k : k + 1]
    out_ref[...] = (hidden[...] + total[...]).astype(bf16)


def shift(steps, count):
    return [(i, (i + steps) % count) for i in range(count)]


def flip(bits):
    return [(i, i ^ bits) for i in range(4)]


def on_device(
    stream_in, queries, keys, values, w_out, norm_gain, expert_ids, gates, w_gate, w_up, w_down
):
    shard, head = queries.shape
    tokens, width = stream_in.shape
    n_ctx = 8
    experts = 64
    hidden_units = w_gate.shape[2]
    quarter = width // 4
    place = lax.axis_index("xh") * 4 + lax.axis_index("y")
    quad = lax.axis_index(QUAD)

    weights = []
    for d in range(4):
        cols = lax.dynamic_slice_in_dim(w_out, (quad ^ d) * quarter, quarter, 1)
        weights.append(cols if d == 0 else lax.ppermute(cols, QUAD, flip(d)))

    copies = pl.pallas_call(
        pack_kernel,
        out_shape=jax.ShapeDtypeStruct((n_ctx, shard, 2 * head), bf16),
        in_specs=[VMEM, VMEM],
        out_specs=ANY,
        scratch_shapes=[pltpu.VMEM((shard, 2 * head), bf16), pltpu.SemaphoreType.DMA((n_ctx,))],
        compiler_params=pltpu.CompilerParams(vmem_limit_bytes=8 * 1024 * 1024),
        name="pack",
    )(keys, values)
    everyone = lax.all_to_all(copies, CTX, 0, 0, tiled=True)
    attended = pl.pallas_call(
        attention_kernel,
        out_shape=jax.ShapeDtypeStruct((shard, head), bf16),
        in_specs=[SMEM, VMEM, ANY],
        out_specs=VMEM,
        scratch_shapes=[
            pltpu.VMEM((n_ctx, shard, 2 * head), bf16),
            pltpu.SemaphoreType.DMA((n_ctx,)),
        ],
        compiler_params=pltpu.CompilerParams(vmem_limit_bytes=8 * 1024 * 1024),
        name="attention",
    )(place.reshape(1).astype(jnp.int32), queries, everyone)

    heads = [attended] + [lax.ppermute(attended, QUAD, flip(d)) for d in (1, 2, 3)]
    term = pl.pallas_call(
        project_kernel,
        out_shape=jax.ShapeDtypeStruct((shard, quarter), bf16),
        in_specs=[VMEM] * 8,
        out_specs=VMEM,
        compiler_params=pltpu.CompilerParams(vmem_limit_bytes=8 * 1024 * 1024),
        name="project",
    )(*heads, *weights)
    terms = lax.all_to_all(term.reshape(-1, tokens, quarter), EXP, 0, 0, tiled=True)

    slots = 2 * experts
    hidden, outgoing = pl.pallas_call(
        dispatch_kernel,
        out_shape=(
            jax.ShapeDtypeStruct((tokens, width), f32),
            jax.ShapeDtypeStruct((slots, SUB, LANE), bf16),
        ),
        in_specs=[SMEM, VMEM, VMEM, VMEM],
        out_specs=(VMEM, VMEM),
        scratch_shapes=[
            pltpu.SMEM((experts,), jnp.int32),
            pltpu.VMEM((tokens, SUB, LANE), bf16),
        ],
        compiler_params=pltpu.CompilerParams(vmem_limit_bytes=8 * 1024 * 1024),
        name="dispatch",
    )(expert_ids, terms, stream_in, norm_gain.reshape(1, width))

    def home(rows):
        return lax.all_to_all(rows, HOME, 0, 0, tiled=True)

    def block(rows):
        return jax.ShapeDtypeStruct((rows, SUB, LANE), bf16)

    per = experts
    def expert_call(sizes_out, *inputs):
        sizes_in = tuple(x.shape[0] for x in inputs)
        total = sum(sizes_in)
        weight = pltpu.VMEM((hidden_units, width), bf16)
        return pl.pallas_call(
            functools.partial(expert_kernel, sizes_in, sizes_out),
            out_shape=tuple(block(size) for size in sizes_out),
            in_specs=[ANY] * (len(inputs) + 3),
            out_specs=(ANY,) * len(sizes_out),
            scratch_shapes=[
                pltpu.VMEM((total, SUB, LANE), bf16),
                weight,
                weight,
                weight,
                pltpu.VMEM((total, width), bf16),
                pltpu.VMEM((total // SUB, SUB * SUB, LANE), bf16),
                pltpu.VMEM((total, SUB, LANE), bf16),
                pltpu.SemaphoreType.DMA((len(sizes_in),)),
                pltpu.SemaphoreType.DMA((3,)),
                pltpu.SemaphoreType.DMA((len(sizes_out),)),
            ],
            compiler_params=pltpu.CompilerParams(vmem_limit_bytes=62 * 1024 * 1024),
            cost_estimate=pl.CostEstimate(
                flops=6 * total * hidden_units * width,
                bytes_accessed=6 * hidden_units * width,
                transcendentals=0,
            ),
            name="experts",
        )(*inputs, w_gate[0, 0], w_up[0, 0], w_down[0, 0])

    def up(rows):
        return lax.ppermute(rows, "y", shift(1, 4))

    def down(rows):
        return lax.ppermute(rows, "y", shift(-1, 4))

    arrived = home(outgoing.reshape(experts, 2 * SUB, LANE)).reshape(slots, SUB, LANE)
    head, tail = arrived[:per], arrived[per:]
    near = (up(head), down(tail), up(tail), down(head))
    (own,) = expert_call((slots,), arrived)
    (below_head, above_tail, below_tail, above_head), own = lax.optimization_barrier((near, own))
    far = (up(below_head), down(above_tail))
    early = expert_call((per,) * 4, below_head, below_tail, above_head, above_tail)
    early, far = lax.optimization_barrier((early, far))
    ready = (down(early[0]), up(early[3]))
    late = expert_call((per, per), *far)
    ready, late = lax.optimization_barrier((ready, late))
    sum_below, sum_above = pl.pallas_call(
        relay_kernel,
        out_shape=(block(per), block(per)),
        in_specs=[VMEM] * 4,
        out_specs=(VMEM, VMEM),
        compiler_params=pltpu.CompilerParams(vmem_limit_bytes=8 * 1024 * 1024),
        name="relay",
    )(early[1], down(late[1]), early[2], up(late[0]))
    rest = (down(sum_below), up(sum_above))
    part = per // 2

    def part_at(first):
        return pl.BlockSpec((part, SUB, LANE), lambda i: (i + first, 0, 0))

    totals = pl.pallas_call(
        total_kernel,
        grid=(2,),
        out_shape=jax.ShapeDtypeStruct((2, per, SUB, LANE), bf16),
        in_specs=[part_at(0)] * 3 + [part_at(2), part_at(0), part_at(0)],
        out_specs=pl.BlockSpec((2, part, SUB, LANE), lambda i: (0, i, 0, 0)),
        compiler_params=pltpu.CompilerParams(vmem_limit_bytes=12 * 1024 * 1024),
        name="totals",
    )(own, ready[0], rest[1], own, rest[0], ready[1])
    totals = totals.reshape(experts, 2 * SUB, LANE)
    returned = home(totals)

    return pl.pallas_call(
        combine_kernel,
        out_shape=jax.ShapeDtypeStruct((tokens, width), bf16),
        in_specs=[SMEM, SMEM, VMEM, VMEM],
        out_specs=VMEM,
        scratch_shapes=[pltpu.SMEM((experts,), jnp.int32), pltpu.VMEM((tokens, width), f32)],
        compiler_params=pltpu.CompilerParams(vmem_limit_bytes=8 * 1024 * 1024),
        name="combine",
    )(expert_ids, gates, hidden, returned)


def solution(mesh):
    fine = Mesh(mesh.devices.reshape(2, 4, 8, 2, 2), ("xh", "y", "z", "xl", "core"))
    token = CTX + EXP
    placed = (
        P(token, None),
        P(CTX, EXP),
        P(CTX, EXP),
        P(CTX, EXP),
        P(EXP, None),
        P(),
        P(token, None),
        P(token, None),
        P(CTX, EXP, None, None),
        P(CTX, EXP, None, None),
        P(CTX, EXP, None, None),
    )
    return jax.shard_map(
        on_device, mesh=fine, in_specs=placed, out_specs=P(token, None), check_vma=False
    )
```
